128 devices in a mesh: sect: 8 (over x, y_hi), dev: 16 (over y_lo, z, core).
Axes of the slice: x: 4, y: 4 (y_hi: 2, y_lo: 2; y = y_hi * 2 + y_lo), z: 4, core: 2. Of those that a mesh axis runs over, the one named last changes fastest.
Arguments:
- voltages: bfloat16 [2, 2048, 131072], P(None, 'sect', 'dev'), may hold values from -6 to 6
- filter_taps: float32 [4, 1024], replicated, may hold values from -3 to 3
- feed_tile: int32 [2048], P('sect'), may hold values from 0 to 127
- bad_feed: int32 [2048], P('sect'), may hold values 0 or 1
- delays: float32 [1024, 128], P('sect'), may hold values from -32 to 32
Outputs:
- visibilities: float32 [2, 1024, 128, 128], P(None, 'dev', 'sect')
- beams: bfloat16 [2, 1024, 1024, 128], P(None, 'dev', 'sect')
The draws below stay inside these ranges and needn't reach their ends.
Inputs may be any that keep to these rules, and one draw needn't show every extreme that they name: `feed_tile`: each feed belongs to one tile.
All inputs are finite; a program needn't handle non-finite values. No bound on the sum of `bad_feed` on one device may be relied on, other than what follows from the above.
Results may differ from the reference program's by a relative error of at most 0.014.
Values may be sent and summed in bfloat16 or wider, within the bound.
No kernel may reach another device: no remote copies, remote signals or barrier semaphores. Data moves between devices by JAX's collectives and lax.ppermute only.
A program may use at most 192 MiB of HBM per device.

```python
import math
import jax
import jax.numpy as jnp
from jax import lax

FEEDS = 2048
CHANNELS = 1024
TILES = 128
BEAMS = 1024
TAPS = 4
FRAMES = 128
SAMPLES = 131072
N_SECT = 8


def place_ends(entries, rng, low, top_value):
    extent = entries.shape
    index_at = [jax.random.randint(jax.random.fold_in(rng, axis), (), 0, extent[axis]) for axis in range(len(extent))]
    entries = entries.at[tuple(index_at)].set(low)
    longest = extent.index(max(extent))
    index_at[longest] = (index_at[longest] + 1) % extent[longest]
    return entries.at[tuple(index_at)].set(top_value)


def steps_of(key, dims, shards, low, largest):
    factor_of = 1.0
    for dim, parts in shards:
        draws = jax.random.uniform(jax.random.fold_in(jax.random.fold_in(key, 6), dim), (parts,), jnp.float32, low / len(shards), largest / len(shards))
        factor_of = factor_of * jnp.repeat(jnp.exp(draws), dims[dim] // parts).reshape((-1,) + (1,) * (len(dims) - 1 - dim))
    return factor_of


def bell_draw(key, dims, scale, bound, shards=(), kind=jnp.bfloat16):
    gain = steps_of(key, dims, shards, -0.22, 0.18) if shards else 1.0
    drawn = jax.random.normal(key, dims, jnp.float32) * scale * gain
    return jnp.minimum(jnp.maximum(drawn, -bound), bound).astype(kind)


def setup_inputs(seed: int = 0) -> dict:
    key_list = jax.random.split(jax.random.key(seed), 6)
    voltages = bell_draw(key_list[0], (2, FEEDS, SAMPLES), 1.0, 6.0, ((1, 8), (2, 16)))
    filter_taps = bell_draw(key_list[1], (TAPS, CHANNELS), 0.5, 3.0, (), jnp.float32)
    feed_tile = place_ends(jax.random.randint(key_list[2], (FEEDS,), 0, TILES), jax.random.fold_in(key_list[2], 1), 0, TILES - 1).astype(jnp.int32)
    bad_feed = place_ends((jax.random.randint(key_list[3], (FEEDS,), 0, 8) < 1).astype(jnp.int32), jax.random.fold_in(key_list[3], 1), 0, 1)
    delays = jnp.clip(jax.random.uniform(key_list[4], (BEAMS, TILES), jnp.float32, -32.0, 32.0) * steps_of(key_list[4], (BEAMS, TILES), ((0, 8),), -0.4, 0.0), -32.0, 32.0)
    return {"voltages": voltages, "filter_taps": filter_taps, "feed_tile": feed_tile, "bad_feed": bad_feed, "delays": delays}


def fourier_tables():
    positions = jnp.arange(CHANNELS, dtype=jnp.int32)
    product = positions[:, None] * positions[None, :] % CHANNELS
    phase_angle = product.astype(jnp.float32) * (2.0 * math.pi / CHANNELS)
    factor = 1.0 / math.sqrt(CHANNELS)
    cosine_table = (jnp.cos(phase_angle) * factor).astype(jnp.bfloat16)
    sine_table = (jnp.sin(phase_angle) * factor).astype(jnp.bfloat16)
    return (cosine_table, sine_table)

def filter_bank(window, filter_taps, frames):
    running = jnp.zeros((2, window.shape[1], frames, window.shape[3]), jnp.float32)
    for tap_index in range(TAPS):
        begin_frame = TAPS - 1 - tap_index
        running = running + filter_taps[tap_index] * window[:, :, begin_frame:begin_frame + frames].astype(jnp.float32)
    return running.astype(jnp.bfloat16)

def transform(filtered, cosine_table, sine_table):
    real_part = jnp.dot(filtered[0], cosine_table, preferred_element_type=jnp.float32) + jnp.dot(filtered[1], sine_table, preferred_element_type=jnp.float32)
    quad_part = jnp.dot(filtered[1], cosine_table, preferred_element_type=jnp.float32) - jnp.dot(filtered[0], sine_table, preferred_element_type=jnp.float32)
    return jnp.stack([real_part, quad_part]).astype(jnp.bfloat16)

def tile_matrix(feed_tile, bad_feed):
    tile_ids = jnp.arange(TILES, dtype=jnp.int32)
    member = (feed_tile[:, None] == tile_ids[None, :]) & (bad_feed[:, None] == 0)
    return jnp.where(member, 1.0, 0.0).astype(jnp.bfloat16)

def reference(voltages, filter_taps, feed_tile, bad_feed, delays):
    cosine_table, sine_table = fourier_tables()
    block_feeds = FEEDS // N_SECT

    def add_section(section, running):
        first_feed = (section * block_feeds).astype(jnp.int32)
        block = lax.dynamic_slice_in_dim(voltages, first_feed, block_feeds, 1)
        block = block.reshape(2, block_feeds, FRAMES, CHANNELS)
        window = jnp.pad(block, ((0, 0), (0, 0), (TAPS - 1, 0), (0, 0)))
        spectra = transform(filter_bank(window, filter_taps, FRAMES), cosine_table, sine_table)
        matrix = tile_matrix(lax.dynamic_slice_in_dim(feed_tile, first_feed, block_feeds, 0), lax.dynamic_slice_in_dim(bad_feed, first_feed, block_feeds, 0))
        partial_value = jnp.einsum('zfnc,fa->zanc', spectra.astype(jnp.float32), matrix.astype(jnp.float32))
        rounded = lax.optimization_barrier(partial_value.astype(jnp.bfloat16))
        return running + rounded.astype(jnp.float32)
    initial = jnp.zeros((2, TILES, FRAMES, CHANNELS), jnp.float32)
    running = lax.fori_loop(0, N_SECT, add_section, initial)
    tile_volts = running.astype(jnp.bfloat16)
    volts_real = tile_volts[0].astype(jnp.float32)
    volts_quad = tile_volts[1].astype(jnp.float32)
    vis_scale = 1.0 / (FRAMES * FEEDS / TILES)
    real_part = jnp.einsum('atc,btc->cab', volts_real, volts_real) + jnp.einsum('atc,btc->cab', volts_quad, volts_quad)
    quad_part = jnp.einsum('atc,btc->cab', volts_quad, volts_real) - jnp.einsum('atc,btc->cab', volts_real, volts_quad)
    visibilities = jnp.stack([real_part, quad_part]) * vis_scale
    channel = jnp.arange(CHANNELS, dtype=jnp.int32).astype(jnp.float32)
    block_beams = BEAMS // N_SECT

    def beam_block(section):
        delay_rows = lax.dynamic_slice_in_dim(delays, (section * block_beams).astype(jnp.int32), block_beams, 0)
        phase_angle = delay_rows[None, :, :] * channel[:, None, None] * (2.0 * math.pi / CHANNELS)
        weight_cos = jnp.cos(phase_angle).astype(jnp.bfloat16).astype(jnp.float32)
        weight_sin = jnp.sin(phase_angle).astype(jnp.bfloat16).astype(jnp.float32)
        beam_real = jnp.einsum('cba,atc->cbt', weight_cos, volts_real) + jnp.einsum('cba,atc->cbt', weight_sin, volts_quad)
        beam_quad = jnp.einsum('cba,atc->cbt', weight_cos, volts_quad) - jnp.einsum('cba,atc->cbt', weight_sin, volts_real)
        return jnp.stack([beam_real, beam_quad])
    stacked = lax.map(beam_block, jnp.arange(N_SECT, dtype=jnp.int32))
    beams = jnp.transpose(stacked, (1, 2, 0, 3, 4)).reshape(2, CHANNELS, BEAMS, FRAMES)
    beams = (beams * (1.0 / math.sqrt(FEEDS))).astype(jnp.bfloat16)
    return (visibilities, beams)
```

```python
import functools
import math

import jax
import jax.numpy as jnp
import numpy as np
from jax import lax
from jax.experimental import pallas as pl
from jax.experimental.pallas import tpu as pltpu
from jax.sharding import Mesh
from jax.sharding import PartitionSpec as P

FEEDS = 2048
CHANNELS = 1024
TILES = 128
TAPS = 4
FRAMES = 128

SECT = ("x", "yh")
DEV = ("yl", "z", "core")
NX = 4
PER = 16
LOCAL_FRAMES = 8
LATE = 3
EARLY = LOCAL_FRAMES - LATE
LOCAL_CHANS = 64
FIRST = 36
STEP = 4
BF16 = jnp.bfloat16
F32 = jnp.float32


def ring(v, by):
    return lax.ppermute(v, "x", [(i, (i + by) % NX) for i in range(NX)])


def pair(v):
    return lax.ppermute(v, "yh", [(0, 1), (1, 0)])


def add(*terms):
    total = terms[0].astype(F32)
    for term in terms[1:]:
        total = total + term.astype(F32)
    return total.astype(BF16)


def params(**kw):
    return pltpu.CompilerParams(vmem_limit_bytes=48 * 1024 * 1024, **kw)


def tile_sums_kernel(groups, place_ref, volts_ref, *out_refs):
    rows = lax.broadcasted_iota(jnp.int32, (TILES, place_ref.shape[1]), 0)
    member = jnp.where(rows == place_ref[...], 1.0, 0.0).astype(BF16)
    sums = jnp.dot(member, volts_ref[0], preferred_element_type=F32).astype(BF16)
    for out_ref, group in zip(out_refs, groups):
        for place, block in enumerate(group):
            out_ref[place, 0, 0] = sums[block * PER : (block + 1) * PER]


def tile_sums(place, voltages, first, frames, groups):
    feeds = voltages.shape[1]
    return pl.pallas_call(
        functools.partial(tile_sums_kernel, groups),
        grid=(frames, 2),
        in_specs=[
            pl.BlockSpec((1, feeds), lambda t, z: (0, 0)),
            pl.BlockSpec((1, feeds, CHANNELS), lambda t, z: (z, 0, first + t)),
        ],
        out_specs=[
            pl.BlockSpec((len(g), 1, 1, PER, CHANNELS), lambda t, z: (0, t, z, 0, 0)) for g in groups
        ],
        out_shape=[jax.ShapeDtypeStruct((len(g), frames, 2, PER, CHANNELS), BF16) for g in groups],
        compiler_params=params(),
        cost_estimate=pl.CostEstimate(
            flops=2 * TILES * feeds * CHANNELS * 2 * frames,
            bytes_accessed=2 * 2 * frames * CHANNELS * (feeds + TILES),
            transcendentals=0,
        ),
    )(place, voltages)


def spectra_kernel(early_ref, late_ref, past_ref, taps_ref, cos_ref, sin_ref, out_ref, filt_ref):
    @pl.when(pl.program_id(0) == 0)
    def _():
        def frame(t, z):
            if t < 0:
                return past_ref[t + LATE, z].astype(F32)
            if t < EARLY:
                return early_ref[t, z].astype(F32)
            return late_ref[t - EARLY, z].astype(F32)

        for z in range(2):
            for t in range(LOCAL_FRAMES):
                total = taps_ref[0:1, :] * frame(t - 0, z)
                for m in range(1, TAPS):
                    total = total + taps_ref[m : m + 1, :] * frame(t - m, z)
                filt_ref[z * TILES + t * PER : z * TILES + (t + 1) * PER, :] = total.astype(BF16)

    dims = (((1,), (1,)), ((), ()))
    by_cos = lax.dot_general(cos_ref[...], filt_ref[...], dims, preferred_element_type=F32)
    by_sin = lax.dot_general(sin_ref[...], filt_ref[...], dims, preferred_element_type=F32)
    out_ref[:, 0:128] = (by_cos[:, 0:128] + by_sin[:, 128:256]).astype(BF16)
    out_ref[:, 128:256] = (by_cos[:, 128:256] - by_sin[:, 0:128]).astype(BF16)


def spectra(early, late, past, taps, cos_table, sin_table):
    whole4 = lambda i: (0, 0, 0, 0)
    block = 256
    return pl.pallas_call(
        spectra_kernel,
        grid=(CHANNELS // block,),
        in_specs=[
            pl.BlockSpec((EARLY, 2, PER, CHANNELS), whole4),
            pl.BlockSpec((LATE, 2, PER, CHANNELS), whole4),
            pl.BlockSpec((LATE, 2, PER, CHANNELS), whole4),
            pl.BlockSpec((TAPS, CHANNELS), lambda i: (0, 0)),
            pl.BlockSpec((block, CHANNELS), lambda i: (i, 0)),
            pl.BlockSpec((block, CHANNELS), lambda i: (i, 0)),
        ],
        out_specs=pl.BlockSpec((block, 256), lambda i: (i, 0)),
        out_shape=jax.ShapeDtypeStruct((CHANNELS, 256), BF16),
        scratch_shapes=[pltpu.VMEM((256, CHANNELS), BF16)],
        compiler_params=params(),
        cost_estimate=pl.CostEstimate(
            flops=2 * 2 * 256 * CHANNELS * CHANNELS, bytes_accessed=6 * 1024 * 1024, transcendentals=0
        ),
    )(early, late, past, taps, cos_table, sin_table)


def products_kernel(places_ref, weight_ref, *refs):
    first_refs, second_refs, (vis_ref, beam_ref, both_ref) = refs[:8], refs[8:16], refs[16:]
    step = pl.program_id(0)

    def fill(block_refs):
        for n, block_ref in enumerate(block_refs):
            row = pl.multiple_of(places_ref[n] * PER, PER)
            for c in range(STEP):
                real, quad = block_ref[c, 0], block_ref[c, 1]
                both_ref[c, pl.ds(row, PER), 0:128] = real
                both_ref[c, pl.ds(row, PER), 128:256] = quad
                both_ref[c, pl.ds(TILES + row, PER), 0:128] = quad
                both_ref[c, pl.ds(TILES + row, PER), 128:256] = -real

    @pl.when(step < FIRST // STEP)
    def _():
        fill(first_refs)

    @pl.when(step >= FIRST // STEP)
    def _():
        fill(second_refs)

    vis_scale = 1.0 / (FRAMES * FEEDS / TILES)
    beam_scale = 1.0 / math.sqrt(FEEDS)
    own = pl.multiple_of(places_ref[0] * PER, PER)
    dims = (((1,), (1,)), ((), ()))
    for c in range(STEP):
        beams = jnp.dot(weight_ref[c], both_ref[c], preferred_element_type=F32) * beam_scale
        beam_ref[0, c] = beams[:, 0:128].astype(BF16)
        beam_ref[1, c] = beams[:, 128:256].astype(BF16)
        every = both_ref[c, 0:TILES]
        for z in range(2):
            mine = both_ref[c, pl.ds(z * TILES + own, PER)]
            vis_ref[z, c] = lax.dot_general(mine, every, dims, preferred_element_type=F32) * vis_scale


def products(places, weights, first, second):
    steps = LOCAL_CHANS // STEP
    firsts = FIRST // STEP
    block = (STEP, 2, PER, FRAMES)
    beams = weights.shape[1]
    return pl.pallas_call(
        products_kernel,
        grid_spec=pltpu.PrefetchScalarGridSpec(
            num_scalar_prefetch=1,
            grid=(steps,),
            in_specs=[pl.BlockSpec((STEP, beams, 2 * TILES), lambda i, p: (i, 0, 0))]
            + [pl.BlockSpec(block, lambda i, p: (jnp.minimum(i, firsts - 1), 0, 0, 0))] * 8
            + [pl.BlockSpec(block, lambda i, p: (jnp.maximum(i - firsts, 0), 0, 0, 0))] * 8,
            out_specs=[
                pl.BlockSpec((2, STEP, PER, TILES), lambda i, p: (0, i, 0, 0)),
                pl.BlockSpec((2, STEP, beams, FRAMES), lambda i, p: (0, i, 0, 0)),
            ],
            scratch_shapes=[pltpu.VMEM((STEP, 2 * TILES, 256), BF16)],
        ),
        out_shape=[
            jax.ShapeDtypeStruct((2, LOCAL_CHANS, PER, TILES), F32),
            jax.ShapeDtypeStruct((2, LOCAL_CHANS, beams, FRAMES), BF16),
        ],
        compiler_params=params(),
        cost_estimate=pl.CostEstimate(
            flops=2 * LOCAL_CHANS * 160 * 256 * 256, bytes_accessed=14 * 1024 * 1024, transcendentals=0
        ),
    )(places, weights, *first, *second)


def reduce_sections(place, voltages):
    keep, give = tile_sums(place, voltages, EARLY, LATE, ((0, 2, 4, 6), (1, 3, 5, 7)))
    got = pair(give)
    x_plus, x_minus, x_next, x_prev, x_own = tile_sums(
        place, voltages, 0, EARLY, ((4, 3), (5, 6), (2,), (7,), (0, 1))
    )
    from_minus, from_plus = ring(x_plus, 1), ring(x_minus, -1)
    last_minus = ring(add(x_next[0], from_minus[0]), 1)
    last_plus = ring(add(x_prev[0], from_plus[0]), -1)
    early_own = add(x_own[0], last_minus, from_plus[1])
    early_give = add(x_own[1], last_plus, from_minus[1])
    early = add(early_own, pair(early_give))

    kept = add(keep, got)
    y_plus = jnp.stack([kept[2][:, 0], kept[1][:, 1]])
    y_minus = jnp.stack([kept[2][:, 1], kept[3][:, 0]])
    from_minus, from_plus = ring(y_plus, 1), ring(y_minus, -1)
    last_minus = ring(add(kept[1][:, 0], from_minus[0]), 1)
    last_plus = ring(add(kept[3][:, 1], from_plus[0]), -1)
    late = jnp.stack(
        [
            add(kept[0][:, 0], last_minus, from_plus[1]),
            add(kept[0][:, 1], last_plus, from_minus[1]),
        ],
        axis=1,
    )
    return early, late


def gather_sections(own):
    first, second = own[:FIRST], own[FIRST:]
    first_pair = pair(first)
    own_minus, own_plus = ring(first, 1), ring(first, -1)
    pair_minus, pair_plus = ring(first_pair, 1), ring(first_pair, -1)
    own_far, pair_far = ring(own_minus, 1), ring(pair_plus, -1)
    firsts = (first, first_pair, own_plus, pair_plus, own_far, pair_far, own_minus, pair_minus)

    half = second.shape[0] // 2
    x_minus, x_plus = ring(second, 1), ring(second, -1)
    x_far = jnp.concatenate([ring(x_minus[:half], 1), ring(x_plus[half:], -1)])
    mine = (second, x_plus, x_far, x_minus)
    theirs = [pair(v) for v in mine]
    seconds = [v for both in zip(mine, theirs) for v in both]
    return firsts, seconds


def fourier_tables():
    positions = np.arange(CHANNELS, dtype=np.int64)
    angle = (positions[:, None] * positions[None, :] % CHANNELS) * (2.0 * math.pi / CHANNELS)
    factor = 1.0 / math.sqrt(CHANNELS)
    cos_table = (np.cos(angle) * factor).astype(np.float32).astype(BF16)
    sin_table = (np.sin(angle) * factor).astype(np.float32).astype(BF16)
    return jnp.asarray(cos_table), jnp.asarray(sin_table)


def local(voltages, filter_taps, feed_tile, bad_feed, delays):
    x, y = lax.axis_index("x"), lax.axis_index("yh")
    section = feed_tile // PER
    place = (((section // 2 - x) % NX) * 2 + (section % 2 ^ y)) * PER + feed_tile % PER
    place = jnp.where(bad_feed == 0, place, -1)[None, :]
    cos_table, sin_table = fourier_tables()

    channel = (lax.axis_index(DEV) * LOCAL_CHANS + jnp.arange(LOCAL_CHANS, dtype=jnp.int32)).astype(F32)
    phase = delays[None, :, :] * channel[:, None, None] * (2.0 * math.pi / CHANNELS)
    weights = jnp.concatenate([jnp.cos(phase).astype(BF16), jnp.sin(phase).astype(BF16)], axis=2)

    early, late = reduce_sections(place, voltages)
    past = lax.ppermute(late, DEV, [(i, i + 1) for i in range(FRAMES // LOCAL_FRAMES - 1)])
    spec = spectra(early, late, past, filter_taps, cos_table, sin_table)
    turned = lax.all_to_all(spec.reshape(16, LOCAL_CHANS, 2, TILES), DEV, 0, 0, tiled=True)
    turned = turned.reshape(16, LOCAL_CHANS, 2, LOCAL_FRAMES, PER)
    own = jnp.transpose(turned, (1, 2, 4, 0, 3)).reshape(LOCAL_CHANS, 2, PER, FRAMES)
    firsts, seconds = gather_sections(own)
    rel = jnp.arange(8, dtype=jnp.int32)
    places = ((x + rel // 2) % NX) * 2 + (rel % 2 ^ y)
    return tuple(products(places.astype(jnp.int32), weights, firsts, seconds))


def solution(mesh):
    fine = Mesh(mesh.devices.reshape(NX, 2, 2, 4, 2), SECT + DEV)
    return jax.shard_map(
        local,
        mesh=fine,
        in_specs=(P(None, SECT, DEV), P(), P(SECT), P(SECT), P(SECT, None)),
        out_specs=(P(None, DEV, SECT, None), P(None, DEV, SECT, None)),
        check_vma=False,
    )
```

```python
import functools
import math

import jax
import jax.numpy as jnp
import numpy as np
from jax import lax
from jax.experimental import pallas as pl
from jax.experimental.pallas import tpu as pltpu
from jax.sharding import Mesh
from jax.sharding import PartitionSpec as P

FEEDS = 2048
CHANNELS = 1024
TILES = 128
TAPS = 4
FRAMES = 128

SECT = ("x", "yh")
DEV = ("yl", "z", "core")
NX = 4
PER = 16
LOCAL_FRAMES = 8
LATE = 3
EARLY = LOCAL_FRAMES - LATE
LOCAL_CHANS = 64
FIRST = 40
STEP = 4
BF16 = jnp.bfloat16
F32 = jnp.float32


def ring(v, by):
    return lax.ppermute(v, "x", [(i, (i + by) % NX) for i in range(NX)])


def pair(v):
    return lax.ppermute(v, "yh", [(0, 1), (1, 0)])


def params(mib):
    return pltpu.CompilerParams(vmem_limit_bytes=mib * 1024 * 1024)


IN_VMEM = pl.BlockSpec(memory_space=pltpu.VMEM)
IN_SMEM = pl.BlockSpec(memory_space=pltpu.SMEM)
ANYWHERE = pl.BlockSpec(memory_space=pl.ANY)
IN_HBM = pl.BlockSpec(memory_space=pltpu.HBM)


def combine_kernel(layout, *refs):
    in_refs, out_refs = refs[: -len(layout)], refs[-len(layout) :]
    for out_ref, blocks in zip(out_refs, layout):
        for place, terms in enumerate(blocks):
            values = [in_refs[array][index] for array, index in terms]
            if len(values) > 1:
                total = values[0].astype(F32)
                for value in values[1:]:
                    total = total + value.astype(F32)
                values = [total.astype(BF16)]
            out_ref[place] = values[0]


def combine(arrays, layout, others=()):
    shapes = []
    for blocks in layout:
        array, index = blocks[0][0]
        shapes.append((len(blocks),) + jax.eval_shape(lambda a, index=index: a[index], arrays[array]).shape)
    return pl.pallas_call(
        functools.partial(combine_kernel, layout),
        in_specs=[IN_VMEM] * len(arrays) + [ANYWHERE] * len(others),
        out_specs=[IN_VMEM] * len(layout),
        out_shape=[jax.ShapeDtypeStruct(shape, BF16) for shape in shapes],
        compiler_params=params(4),
        cost_estimate=pl.CostEstimate(flops=1000, bytes_accessed=1000000, transcendentals=0),
    )(*arrays, *others)


def tile_sums_kernel(first, frames, groups, member_ref, volts_ref, *refs):
    out_refs, (chunk_ref, sems) = refs[-2 - len(groups) : -2], refs[-2:]
    copies = [
        pltpu.make_async_copy(
            volts_ref.at[z, :, pl.ds((first + t) * CHANNELS, CHANNELS)],
            chunk_ref.at[t, z],
            sems.at[t, z],
        )
        for t in range(frames)
        for z in range(2)
    ]
    for copy in copies:
        copy.start()
    for t in range(frames):
        for z in range(2):
            copies[t * 2 + z].wait()
            sums = jnp.dot(member_ref[...], chunk_ref[t, z], preferred_element_type=F32).astype(BF16)
            for out_ref, group in zip(out_refs, groups):
                for place, block in enumerate(group):
                    out_ref[place, t, z] = sums[block * PER : (block + 1) * PER]


def tile_sums(member, voltages, first, frames, groups, others=()):
    feeds = voltages.shape[1]
    return pl.pallas_call(
        functools.partial(tile_sums_kernel, first, frames, groups),
        in_specs=[IN_VMEM, IN_HBM] + [ANYWHERE] * len(others),
        out_specs=[IN_VMEM] * len(groups),
        out_shape=[jax.ShapeDtypeStruct((len(g), frames, 2, PER, CHANNELS), BF16) for g in groups],
        scratch_shapes=[
            pltpu.VMEM((frames, 2, feeds, CHANNELS), BF16),
            pltpu.SemaphoreType.DMA((frames, 2)),
        ],
        compiler_params=params(50),
        cost_estimate=pl.CostEstimate(
            flops=2 * TILES * feeds * CHANNELS * 2 * frames,
            bytes_accessed=2 * 2 * frames * CHANNELS * (feeds + TILES) * 2,
            transcendentals=0,
        ),
    )(member, voltages, *others)


def weights_kernel(base_ref, delays_ref, out_ref):
    @pl.loop(0, out_ref.shape[0])
    def _(c):
        channel = (base_ref[0] + c).astype(F32)
        quarters = (delays_ref[...] * channel) * (4.0 / CHANNELS)
        near = jnp.floor(quarters + 0.5)
        rest = quarters - near
        square = rest * rest
        sine = rest * (
            1.5707963267948966
            + square * (-0.6459640975062462 + square * (0.07969262624616703 + square * -0.004681754135318687))
        )
        cosine = 1.0 + square * (
            -1.2337005501361697
            + square * (0.253669507901048 + square * (-0.020863480763353 + square * 0.000919260274839426))
        )
        turn = near.astype(jnp.int32) & 3
        odd = (turn & 1) == 1
        cos_value, sin_value = jnp.where(odd, sine, cosine), jnp.where(odd, cosine, sine)
        cos_value = jnp.where((turn == 1) | (turn == 2), -cos_value, cos_value)
        sin_value = jnp.where(turn >= 2, -sin_value, sin_value)
        out_ref[c, :, 0:TILES] = cos_value.astype(BF16)
        out_ref[c, :, TILES : 2 * TILES] = sin_value.astype(BF16)


def beam_weights(base, delays, count):
    beams = delays.shape[0]
    return pl.pallas_call(
        weights_kernel,
        in_specs=[IN_SMEM, IN_VMEM],
        out_specs=IN_VMEM,
        out_shape=jax.ShapeDtypeStruct((count, beams, 2 * TILES), BF16),
        compiler_params=params(4),
        cost_estimate=pl.CostEstimate(
            flops=1000, bytes_accessed=count * 400 * 1024, transcendentals=0
        ),
    )(jnp.reshape(base, (1,)), delays)


def spectra_kernel(early_refs, late_ref, past_ref, taps_ref, cos_ref, sin_ref, out_ref, filt_ref):
    def frame(t, z):
        if t < 0:
            return past_ref[t + LATE, z].astype(F32)
        if t < EARLY:
            return early_refs[0][0, t, z].astype(F32) + early_refs[1][0, t, z].astype(F32)
        return late_ref[t - EARLY, z].astype(F32)

    @pl.when(pl.program_id(0) == 0)
    def _():
        for z in range(2):
            for t in range(LOCAL_FRAMES):
                total = taps_ref[0:1, :] * frame(t, z)
                for m in range(1, TAPS):
                    total = total + taps_ref[m : m + 1, :] * frame(t - m, z)
                filt_ref[z * TILES + t * PER : z * TILES + (t + 1) * PER, :] = total.astype(BF16)

    by_cos = jnp.dot(filt_ref[...], cos_ref[...], preferred_element_type=F32)
    by_sin = jnp.dot(filt_ref[...], sin_ref[...], preferred_element_type=F32)
    real = by_cos[0:128] + by_sin[128:256]
    quad = by_cos[128:256] - by_sin[0:128]
    for n in range(real.shape[1] // 128):
        lanes = slice(n * 128, (n + 1) * 128)
        own, other = real[:, lanes], quad[:, lanes]
        out_ref[2 * n] = jnp.concatenate([own[:, 0:64], other[:, 0:64]], axis=1).astype(BF16)
        out_ref[2 * n + 1] = jnp.concatenate([own[:, 64:128], other[:, 64:128]], axis=1).astype(BF16)


def spectra(early, late, past, taps, cos_table, sin_table):
    block = 512
    whole = lambda a: pl.BlockSpec(a.shape, lambda i: (0,) * a.ndim)
    columns = pl.BlockSpec((CHANNELS, block), lambda i: (0, i))

    def kernel(own_ref, got_ref, late_ref, past_ref, taps_ref, cos_ref, sin_ref, *refs):
        spectra_kernel((own_ref, got_ref), late_ref, past_ref, taps_ref, cos_ref, sin_ref, *refs[-2:])

    return pl.pallas_call(
        kernel,
        grid=(CHANNELS // block,),
        in_specs=[whole(a) for a in (*early, late, past, taps)] + [columns] * 2,
        out_specs=pl.BlockSpec((block // LOCAL_CHANS, TILES, 128), lambda i: (i, 0, 0)),
        out_shape=jax.ShapeDtypeStruct((CHANNELS // LOCAL_CHANS, TILES, 128), BF16),
        scratch_shapes=[pltpu.VMEM((256, CHANNELS), BF16)],
        compiler_params=params(12),
        cost_estimate=pl.CostEstimate(
            flops=2 * 2 * 256 * CHANNELS * CHANNELS, bytes_accessed=6 * 1024 * 1024, transcendentals=0
        ),
    )(*early, late, past, taps, cos_table, sin_table)


def turn_kernel(in_ref, first_ref, second_ref, wide_ref, turned_ref):
    for d in range(in_ref.shape[0]):
        wide_ref[d * TILES : (d + 1) * TILES] = in_ref[d].astype(F32)
    for a in range(PER):
        turned_ref[pl.ds(a, 128, stride=PER)] = wide_ref[pl.ds(a, 128, stride=PER)].T
    for z in range(2):
        for ref, begin in ((first_ref, 0), (second_ref, FIRST)):
            for c in range(ref.shape[0]):
                row = (z * LOCAL_CHANS + begin + c) * PER
                ref[c, z] = turned_ref[row : row + PER].astype(BF16)


def turn(value):
    return pl.pallas_call(
        turn_kernel,
        in_specs=[IN_VMEM],
        out_specs=[IN_VMEM] * 2,
        out_shape=[jax.ShapeDtypeStruct((n, 2, PER, FRAMES), BF16) for n in (FIRST, LOCAL_CHANS - FIRST)],
        scratch_shapes=[pltpu.VMEM((FRAMES * PER, 128), F32)] * 2,
        compiler_params=params(4),
        cost_estimate=pl.CostEstimate(flops=1000, bytes_accessed=4000000, transcendentals=0),
    )(value)


def products_kernel(begin, blocks, places_ref, weight_ref, block_refs, vis_ref, beam_ref, both_ref, vis_out, beam_out, vis_sem, beam_sem):
    vis_scale = 1.0 / (FRAMES * FEEDS / TILES)
    beam_scale = 1.0 / math.sqrt(FEEDS)
    dims = (((1,), (1,)), ((), ()))
    steps = weight_ref.shape[0] // STEP

    def copies(step):
        here, there = pl.ds(step * STEP, STEP), pl.ds(begin + step * STEP, STEP)
        return [
            pltpu.make_async_copy(source.at[z, here], target.at[z, there], sem.at[z, step])
            for source, target, sem in ((vis_out, vis_ref, vis_sem), (beam_out, beam_ref, beam_sem))
            for z in range(2)
        ]

    @pl.loop(0, steps)
    def _(step):
        for c in range(STEP):
            here = step * STEP + c
            for place, (array, index) in enumerate(blocks):
                row = pl.multiple_of(places_ref[place] * PER, PER)
                real, quad = block_refs[array][index, here, 0], block_refs[array][index, here, 1]
                both_ref[c, pl.ds(row, PER), 0:128] = real
                both_ref[c, pl.ds(row, PER), 128:256] = quad
                both_ref[c, pl.ds(TILES + row, PER), 0:128] = quad
                both_ref[c, pl.ds(TILES + row, PER), 128:256] = -real
        for c in range(STEP):
            here = step * STEP + c
            beams = jnp.dot(weight_ref[here], both_ref[c], preferred_element_type=F32) * beam_scale
            beam_out[0, here] = beams[:, 0:128].astype(BF16)
            beam_out[1, here] = beams[:, 128:256].astype(BF16)
            array, index = blocks[0]
            real, quad = block_refs[array][index, here, 0], block_refs[array][index, here, 1]
            mine = jnp.concatenate(
                [jnp.concatenate([real, quad], axis=1), jnp.concatenate([quad, -real], axis=1)], axis=0
            )
            vis = lax.dot_general(mine, both_ref[c, 0:TILES], dims, preferred_element_type=F32) * vis_scale
            vis_out[0, here] = vis[:PER]
            vis_out[1, here] = vis[PER:]
        for copy in copies(step):
            copy.start()

    @pl.loop(0, steps)
    def _(step):
        for copy in copies(step):
            copy.wait()


def products(places, weights, begin, blocks, results=()):
    arrays, layout = [], []
    for array, index in blocks:
        if not any(array is a for a in arrays):
            arrays.append(array)
        layout.append((next(n for n, a in enumerate(arrays) if a is array), index))
    count, beams = weights.shape[:2]

    def kernel(places_ref, weight_ref, *refs):
        products_kernel(begin, layout, places_ref, weight_ref, refs[: len(arrays)], *refs[len(arrays) + len(results) :])

    return pl.pallas_call(
        kernel,
        in_specs=[IN_SMEM] + [IN_VMEM] * (1 + len(arrays)) + [IN_HBM] * len(results),
        out_specs=[IN_HBM, IN_HBM],
        out_shape=[
            jax.ShapeDtypeStruct((2, LOCAL_CHANS, PER, TILES), F32),
            jax.ShapeDtypeStruct((2, LOCAL_CHANS, beams, FRAMES), BF16),
        ],
        scratch_shapes=[
            pltpu.VMEM((STEP, 2 * TILES, 256), BF16),
            pltpu.VMEM((2, count, PER, TILES), F32),
            pltpu.VMEM((2, count, beams, FRAMES), BF16),
            pltpu.SemaphoreType.DMA((2, count // STEP)),
            pltpu.SemaphoreType.DMA((2, count // STEP)),
        ],
        input_output_aliases={2 + len(arrays) + n: n for n in range(len(results))},
        compiler_params=params(8),
        cost_estimate=pl.CostEstimate(
            flops=2 * count * 160 * 256 * 256, bytes_accessed=count * 400 * 1024, transcendentals=0
        ),
    )(places, weights, *arrays, *results)


def reduce_sections(member, voltages, others):
    x_plus, x_minus, x_rest = tile_sums(member, voltages, 0, EARLY, ((4, 3), (5, 6), (0, 1, 2, 7)))
    keep, give = tile_sums(member, voltages, EARLY, LATE, ((0, 2, 4, 6), (1, 3, 5, 7)), (x_rest,))
    got = pair(give)
    from_minus, from_plus = ring(x_plus, 1), ring(x_minus, -1)
    x_next, x_prev = combine(
        (x_rest, from_minus, from_plus), ([[(0, 2), (1, 0)]], [[(0, 3), (2, 0)]]), others
    )
    last_minus, last_plus = ring(x_next, 1), ring(x_prev, -1)
    early_own, early_give = combine(
        (x_rest, last_minus, last_plus, from_minus, from_plus),
        ([[(0, 0), (1, 0), (4, 1)]], [[(0, 1), (2, 0), (3, 1)]]),
    )
    early = (early_own, pair(early_give))

    y_own, y_next, y_far, y_prev = combine(
        (keep, got), [[[(0, (rx, t)), (1, (rx, t))] for t in range(LATE)] for rx in range(NX)]
    )
    (late,) = combine(
        (y_own, ring(y_next, 1), ring(y_far, 2), ring(y_prev, 3)),
        ([[(n, t) for n in range(NX)] for t in range(LATE)],),
    )
    return early, late


def gather_sections(first, second):
    (both,) = combine((first, pair(first)), ([[(0, slice(None))], [(1, slice(None))]],))
    both_minus, both_plus = ring(both, 1), ring(both, -1)
    own_far, pair_far = ring(both_minus[:1], 1), ring(both_plus[1:], -1)
    firsts = ((both, 0), (both, 1), (both_plus, 0), (both_plus, 1))
    firsts += ((own_far, 0), (pair_far, 0), (both_minus, 0), (both_minus, 1))

    (mine,) = combine(
        (second, ring(second, -1), ring(second, 2), ring(second, 1)), ([[(n, slice(None))] for n in range(NX)],)
    )
    theirs = pair(mine)
    seconds = tuple((v, n) for n in range(NX) for v in (mine, theirs))
    return firsts, seconds


def fourier_tables():
    positions = np.arange(CHANNELS, dtype=np.int64)
    angle = (positions[:, None] * positions[None, :] % CHANNELS) * (2.0 * math.pi / CHANNELS)
    factor = 1.0 / math.sqrt(CHANNELS)
    cos_table = (np.cos(angle) * factor).astype(np.float32).astype(BF16)
    sin_table = (np.sin(angle) * factor).astype(np.float32).astype(BF16)
    return jnp.asarray(cos_table), jnp.asarray(sin_table)


def local(voltages, filter_taps, feed_tile, bad_feed, delays):
    x, y = lax.axis_index("x"), lax.axis_index("yh")
    section = feed_tile // PER
    place = (((section // 2 - x) % NX) * 2 + (section % 2 ^ y)) * PER + feed_tile % PER
    place = jnp.where(bad_feed == 0, place, -1)
    member = (jnp.arange(TILES, dtype=jnp.int32)[:, None] == place[None, :]).astype(BF16)
    cos_table, sin_table = fourier_tables()
    base = (lax.axis_index(DEV) * LOCAL_CHANS).astype(jnp.int32)
    counts = (FIRST, LOCAL_CHANS - FIRST)
    weights = [beam_weights(base + b, delays, n) for b, n in zip((0, FIRST), counts)]

    early, late = reduce_sections(member, voltages, weights)
    past = lax.ppermute(late, DEV, [(i, i + 1) for i in range(FRAMES // LOCAL_FRAMES - 1)])
    spec = spectra(early, late, past, filter_taps, cos_table, sin_table)
    first, second = turn(lax.all_to_all(spec, DEV, 0, 0, tiled=True))
    rel = jnp.arange(8, dtype=jnp.int32)
    places = ((x + rel // 2) % NX) * 2 + (rel % 2 ^ y)
    places = places.astype(jnp.int32)
    firsts, seconds = gather_sections(first, second)
    results = products(places, weights[1], FIRST, seconds)
    return tuple(products(places, weights[0], 0, firsts, results))


def solution(mesh):
    fine = Mesh(mesh.devices.reshape(NX, 2, 2, 4, 2), SECT + DEV)
    return jax.shard_map(
        local,
        mesh=fine,
        in_specs=(P(None, SECT, DEV), P(), P(SECT), P(SECT), P(SECT, None)),
        out_specs=(P(None, DEV, SECT, None), P(None, DEV, SECT, None)),
        check_vma=False,
    )
```

```python
import functools
import math

import jax
import jax.numpy as jnp
import numpy as np
from jax import lax
from jax.experimental import pallas as pl
from jax.experimental.pallas import tpu as pltpu
from jax.sharding import Mesh
from jax.sharding import PartitionSpec as P

FEEDS = 2048
CHANNELS = 1024
TILES = 128
TAPS = 4
FRAMES = 128

SECT = ("x", "yh")
DEV = ("yl", "z", "core")
NX = 4
PER = 16
LOCAL_FRAMES = 8
LATE = 3
EARLY = LOCAL_FRAMES - LATE
LOCAL_CHANS = 64
FIRST = 40
STEP = 8
BF16 = jnp.bfloat16
F32 = jnp.float32


def ring(v, by):
    return lax.ppermute(v, "x", [(i, (i + by) % NX) for i in range(NX)])


def pair(v):
    return lax.ppermute(v, "yh", [(0, 1), (1, 0)])


def params(mib):
    return pltpu.CompilerParams(vmem_limit_bytes=mib * 1024 * 1024)


IN_VMEM = pl.BlockSpec(memory_space=pltpu.VMEM)
IN_SMEM = pl.BlockSpec(memory_space=pltpu.SMEM)
ANYWHERE = pl.BlockSpec(memory_space=pl.ANY)
IN_HBM = pl.BlockSpec(memory_space=pltpu.HBM)


def combine_kernel(layout, *refs):
    in_refs, out_refs = refs[: -len(layout)], refs[-len(layout) :]
    for out_ref, blocks in zip(out_refs, layout):
        for place, terms in enumerate(blocks):
            values = [in_refs[array][index] for array, index in terms]
            if len(values) > 1:
                total = values[0].astype(F32)
                for value in values[1:]:
                    total = total + value.astype(F32)
                values = [total.astype(BF16)]
            out_ref[place] = values[0]


def combine(arrays, layout, others=()):
    shapes = []
    for blocks in layout:
        array, index = blocks[0][0]
        shapes.append((len(blocks),) + jax.eval_shape(lambda a, index=index: a[index], arrays[array]).shape)
    return pl.pallas_call(
        functools.partial(combine_kernel, layout),
        in_specs=[IN_VMEM] * len(arrays) + [ANYWHERE] * len(others),
        out_specs=[IN_VMEM] * len(layout),
        out_shape=[jax.ShapeDtypeStruct(shape, BF16) for shape in shapes],
        compiler_params=params(4),
        cost_estimate=pl.CostEstimate(flops=1000, bytes_accessed=1000000, transcendentals=0),
    )(*arrays, *others)


def tile_sums_kernel(first, frames, groups, member_ref, volts_ref, *refs):
    out_refs, (chunk_ref, sems) = refs[-2 - len(groups) : -2], refs[-2:]
    copies = [
        pltpu.make_async_copy(
            volts_ref.at[z, :, pl.ds((first + t) * CHANNELS, CHANNELS)],
            chunk_ref.at[t, z],
            sems.at[t, z],
        )
        for t in range(frames)
        for z in range(2)
    ]
    for copy in copies:
        copy.start()
    for t in range(frames):
        for z in range(2):
            copies[t * 2 + z].wait()
            sums = jnp.dot(member_ref[...], chunk_ref[t, z], preferred_element_type=F32).astype(BF16)
            for out_ref, group in zip(out_refs, groups):
                for place, block in enumerate(group):
                    out_ref[place, t, z] = sums[block * PER : (block + 1) * PER]


def tile_sums(member, voltages, first, frames, groups, others=()):
    feeds = voltages.shape[1]
    return pl.pallas_call(
        functools.partial(tile_sums_kernel, first, frames, groups),
        in_specs=[IN_VMEM, IN_HBM] + [ANYWHERE] * len(others),
        out_specs=[IN_VMEM] * len(groups),
        out_shape=[jax.ShapeDtypeStruct((len(g), frames, 2, PER, CHANNELS), BF16) for g in groups],
        scratch_shapes=[
            pltpu.VMEM((frames, 2, feeds, CHANNELS), BF16),
            pltpu.SemaphoreType.DMA((frames, 2)),
        ],
        compiler_params=params(50),
        cost_estimate=pl.CostEstimate(
            flops=2 * TILES * feeds * CHANNELS * 2 * frames,
            bytes_accessed=2 * 2 * frames * CHANNELS * (feeds + TILES) * 2,
            transcendentals=0,
        ),
    )(member, voltages, *others)


def weights_kernel(base_ref, delays_ref, out_ref):
    @pl.loop(0, out_ref.shape[0])
    def _(c):
        channel = (base_ref[0] + c).astype(F32)
        quarters = (delays_ref[...] * channel) * (4.0 / CHANNELS)
        near = jnp.floor(quarters + 0.5)
        rest = quarters - near
        square = rest * rest
        sine = rest * (
            1.5707963267948966
            + square * (-0.6459640975062462 + square * (0.07969262624616703 + square * -0.004681754135318687))
        )
        cosine = 1.0 + square * (
            -1.2337005501361697
            + square * (0.253669507901048 + square * (-0.020863480763353 + square * 0.000919260274839426))
        )
        turn = near.astype(jnp.int32) & 3
        odd = (turn & 1) == 1
        cos_value, sin_value = jnp.where(odd, sine, cosine), jnp.where(odd, cosine, sine)
        cos_value = jnp.where((turn == 1) | (turn == 2), -cos_value, cos_value)
        sin_value = jnp.where(turn >= 2, -sin_value, sin_value)
        out_ref[c, :, 0:TILES] = cos_value.astype(BF16)
        out_ref[c, :, TILES : 2 * TILES] = sin_value.astype(BF16)


def beam_weights(base, delays, count):
    beams = delays.shape[0]
    return pl.pallas_call(
        weights_kernel,
        in_specs=[IN_SMEM, IN_VMEM],
        out_specs=IN_VMEM,
        out_shape=jax.ShapeDtypeStruct((count, beams, 2 * TILES), BF16),
        compiler_params=params(4),
        cost_estimate=pl.CostEstimate(
            flops=1000, bytes_accessed=count * 400 * 1024, transcendentals=0
        ),
    )(jnp.reshape(base, (1,)), delays)


def spectra_kernel(early_refs, late_ref, past_ref, taps_ref, cos_ref, sin_ref, out_ref, filt_ref):
    def frame(t, z):
        if t < 0:
            return past_ref[t + LATE, z].astype(F32)
        if t < EARLY:
            return early_refs[0][0, t, z].astype(F32) + early_refs[1][0, t, z].astype(F32)
        return late_ref[t - EARLY, z].astype(F32)

    @pl.when(pl.program_id(0) == 0)
    def _():
        for z in range(2):
            for t in range(LOCAL_FRAMES):
                total = taps_ref[0:1, :] * frame(t, z)
                for m in range(1, TAPS):
                    total = total + taps_ref[m : m + 1, :] * frame(t - m, z)
                filt_ref[z * TILES + t * PER : z * TILES + (t + 1) * PER, :] = total.astype(BF16)

    by_cos = jnp.dot(filt_ref[...], cos_ref[...], preferred_element_type=F32)
    by_sin = jnp.dot(filt_ref[...], sin_ref[...], preferred_element_type=F32)
    real = by_cos[0:128] + by_sin[128:256]
    quad = by_cos[128:256] - by_sin[0:128]
    for n in range(real.shape[1] // 128):
        lanes = slice(n * 128, (n + 1) * 128)
        own, other = real[:, lanes], quad[:, lanes]
        out_ref[2 * n] = jnp.concatenate([own[:, 0:64], other[:, 0:64]], axis=1).astype(BF16)
        out_ref[2 * n + 1] = jnp.concatenate([own[:, 64:128], other[:, 64:128]], axis=1).astype(BF16)


def spectra(early, late, past, taps, cos_table, sin_table):
    block = 512
    whole = lambda a: pl.BlockSpec(a.shape, lambda i: (0,) * a.ndim)
    columns = pl.BlockSpec((CHANNELS, block), lambda i: (0, i))

    def kernel(own_ref, got_ref, late_ref, past_ref, taps_ref, cos_ref, sin_ref, *refs):
        spectra_kernel((own_ref, got_ref), late_ref, past_ref, taps_ref, cos_ref, sin_ref, *refs[-2:])

    return pl.pallas_call(
        kernel,
        grid=(CHANNELS // block,),
        in_specs=[whole(a) for a in (*early, late, past, taps)] + [columns] * 2,
        out_specs=pl.BlockSpec((block // LOCAL_CHANS, TILES, 128), lambda i: (i, 0, 0)),
        out_shape=jax.ShapeDtypeStruct((CHANNELS // LOCAL_CHANS, TILES, 128), BF16),
        scratch_shapes=[pltpu.VMEM((256, CHANNELS), BF16)],
        compiler_params=params(12),
        cost_estimate=pl.CostEstimate(
            flops=2 * 2 * 256 * CHANNELS * CHANNELS, bytes_accessed=6 * 1024 * 1024, transcendentals=0
        ),
    )(*early, late, past, taps, cos_table, sin_table)


def turn_kernel(in_ref, first_ref, second_ref, wide_ref, turned_ref):
    for d in range(in_ref.shape[0]):
        wide_ref[d * TILES : (d + 1) * TILES] = in_ref[d].astype(F32)
    for a in range(PER):
        turned_ref[pl.ds(a, 128, stride=PER)] = wide_ref[pl.ds(a, 128, stride=PER)].T
    for z in range(2):
        for ref, begin in ((first_ref, 0), (second_ref, FIRST)):
            for c in range(ref.shape[0]):
                row = (z * LOCAL_CHANS + begin + c) * PER
                ref[c, z] = turned_ref[row : row + PER].astype(BF16)


def turn(value):
    return pl.pallas_call(
        turn_kernel,
        in_specs=[IN_VMEM],
        out_specs=[IN_VMEM] * 2,
        out_shape=[jax.ShapeDtypeStruct((n, 2, PER, FRAMES), BF16) for n in (FIRST, LOCAL_CHANS - FIRST)],
        scratch_shapes=[pltpu.VMEM((FRAMES * PER, 128), F32)] * 2,
        compiler_params=params(4),
        cost_estimate=pl.CostEstimate(flops=1000, bytes_accessed=4000000, transcendentals=0),
    )(value)


def products_kernel(begin, blocks, places_ref, weight_ref, block_refs, vis_ref, beam_ref, both_ref, vis_out, beam_out, vis_sem, beam_sem):
    vis_scale = 1.0 / (FRAMES * FEEDS / TILES)
    beam_scale = 1.0 / math.sqrt(FEEDS)
    dims = (((1,), (1,)), ((), ()))
    steps = weight_ref.shape[0] // STEP

    def copies(step):
        here, there = pl.ds(step * STEP, STEP), pl.ds(begin + step * STEP, STEP)
        return [
            pltpu.make_async_copy(source.at[z, here], target.at[z, there], sem.at[z, step])
            for source, target, sem in ((vis_out, vis_ref, vis_sem), (beam_out, beam_ref, beam_sem))
            for z in range(2)
        ]

    @pl.loop(0, steps)
    def _(step):
        for c in range(STEP):
            here = step * STEP + c
            for place, (array, index) in enumerate(blocks):
                row = pl.multiple_of(places_ref[place] * PER, PER)
                real, quad = block_refs[array][index, here, 0], block_refs[array][index, here, 1]
                both_ref[c, pl.ds(row, PER), 0:128] = real
                both_ref[c, pl.ds(row, PER), 128:256] = quad
                both_ref[c, pl.ds(TILES + row, PER), 0:128] = quad
                both_ref[c, pl.ds(TILES + row, PER), 128:256] = -real
        for c in range(STEP):
            here = step * STEP + c
            beams = jnp.dot(weight_ref[here], both_ref[c], preferred_element_type=F32) * beam_scale
            beam_out[0, here] = beams[:, 0:128].astype(BF16)
            beam_out[1, here] = beams[:, 128:256].astype(BF16)
            array, index = blocks[0]
            real, quad = block_refs[array][index, here, 0], block_refs[array][index, here, 1]
            mine = jnp.concatenate(
                [jnp.concatenate([real, quad], axis=1), jnp.concatenate([quad, -real], axis=1)], axis=0
            )
            vis = lax.dot_general(mine, both_ref[c, 0:TILES], dims, preferred_element_type=F32) * vis_scale
            vis_out[0, here] = vis[:PER]
            vis_out[1, here] = vis[PER:]
        for copy in copies(step):
            copy.start()

    @pl.loop(0, steps)
    def _(step):
        for copy in copies(step):
            copy.wait()


def products(places, weights, begin, blocks, results=()):
    arrays, layout = [], []
    for array, index in blocks:
        if not any(array is a for a in arrays):
            arrays.append(array)
        layout.append((next(n for n, a in enumerate(arrays) if a is array), index))
    count, beams = weights.shape[:2]

    def kernel(places_ref, weight_ref, *refs):
        products_kernel(begin, layout, places_ref, weight_ref, refs[: len(arrays)], *refs[len(arrays) + len(results) :])

    return pl.pallas_call(
        kernel,
        in_specs=[IN_SMEM] + [IN_VMEM] * (1 + len(arrays)) + [IN_HBM] * len(results),
        out_specs=[IN_HBM, IN_HBM],
        out_shape=[
            jax.ShapeDtypeStruct((2, LOCAL_CHANS, PER, TILES), F32),
            jax.ShapeDtypeStruct((2, LOCAL_CHANS, beams, FRAMES), BF16),
        ],
        scratch_shapes=[
            pltpu.VMEM((STEP, 2 * TILES, 256), BF16),
            pltpu.VMEM((2, count, PER, TILES), F32),
            pltpu.VMEM((2, count, beams, FRAMES), BF16),
            pltpu.SemaphoreType.DMA((2, count // STEP)),
            pltpu.SemaphoreType.DMA((2, count // STEP)),
        ],
        input_output_aliases={2 + len(arrays) + n: n for n in range(len(results))},
        compiler_params=params(8),
        cost_estimate=pl.CostEstimate(
            flops=2 * count * 160 * 256 * 256, bytes_accessed=count * 400 * 1024, transcendentals=0
        ),
    )(places, weights, *arrays, *results)


def reduce_sections(member, voltages):
    x_plus, x_minus, x_rest = tile_sums(member, voltages, 0, EARLY, ((4, 3), (5, 6), (0, 1, 2, 7)))
    keep, give = tile_sums(member, voltages, EARLY, LATE, ((0, 2, 4, 6), (1, 3, 5, 7)), (x_rest,))
    got = pair(give)
    from_minus, from_plus = ring(x_plus, 1), ring(x_minus, -1)
    x_next, x_prev = combine(
        (x_rest, from_minus, from_plus), ([[(0, 2), (1, 0)]], [[(0, 3), (2, 0)]])
    )
    last_minus, last_plus = ring(x_next, 1), ring(x_prev, -1)
    early_own, early_give = combine(
        (x_rest, last_minus, last_plus, from_minus, from_plus),
        ([[(0, 0), (1, 0), (4, 1)]], [[(0, 1), (2, 0), (3, 1)]]),
    )
    early = (early_own, pair(early_give))

    y_own, y_next, y_far, y_prev = combine(
        (keep, got), [[[(0, (rx, t)), (1, (rx, t))] for t in range(LATE)] for rx in range(NX)]
    )
    (late,) = combine(
        (y_own, ring(y_next, 1), ring(y_far, 2), ring(y_prev, 3)),
        ([[(n, t) for n in range(NX)] for t in range(LATE)],),
    )
    return early, late


def gather_sections(first, second, others):
    (both,) = combine((first, pair(first)), ([[(0, slice(None))], [(1, slice(None))]],))
    both_minus, both_plus = ring(both, 1), ring(both, -1)
    own_far, pair_far = combine((both_minus, both_plus), ([[(0, 0)]], [[(1, 1)]]), others)
    own_far, pair_far = ring(own_far, 1), ring(pair_far, -1)
    firsts = ((both, 0), (both, 1), (both_plus, 0), (both_plus, 1))
    firsts += ((own_far, 0), (pair_far, 0), (both_minus, 0), (both_minus, 1))

    (mine,) = combine(
        (second, ring(second, -1), ring(second, 2), ring(second, 1)), ([[(n, slice(None))] for n in range(NX)],)
    )
    theirs = pair(mine)
    seconds = tuple((v, n) for n in range(NX) for v in (mine, theirs))
    return firsts, seconds


def fourier_tables():
    positions = np.arange(CHANNELS, dtype=np.int64)
    angle = (positions[:, None] * positions[None, :] % CHANNELS) * (2.0 * math.pi / CHANNELS)
    factor = 1.0 / math.sqrt(CHANNELS)
    cos_table = (np.cos(angle) * factor).astype(np.float32).astype(BF16)
    sin_table = (np.sin(angle) * factor).astype(np.float32).astype(BF16)
    return jnp.asarray(cos_table), jnp.asarray(sin_table)


def local(voltages, filter_taps, feed_tile, bad_feed, delays):
    x, y = lax.axis_index("x"), lax.axis_index("yh")
    section = feed_tile // PER
    place = (((section // 2 - x) % NX) * 2 + (section % 2 ^ y)) * PER + feed_tile % PER
    place = jnp.where(bad_feed == 0, place, -1)
    member = (jnp.arange(TILES, dtype=jnp.int32)[:, None] == place[None, :]).astype(BF16)
    cos_table, sin_table = fourier_tables()
    base = (lax.axis_index(DEV) * LOCAL_CHANS).astype(jnp.int32)
    counts = (FIRST, LOCAL_CHANS - FIRST)
    weights = [beam_weights(base + b, delays, n) for b, n in zip((0, FIRST), counts)]

    early, late = reduce_sections(member, voltages)
    past = lax.ppermute(late, DEV, [(i, i + 1) for i in range(FRAMES // LOCAL_FRAMES - 1)])
    spec = spectra(early, late, past, filter_taps, cos_table, sin_table)
    first, second = turn(lax.all_to_all(spec, DEV, 0, 0, tiled=True))
    rel = jnp.arange(8, dtype=jnp.int32)
    places = ((x + rel // 2) % NX) * 2 + (rel % 2 ^ y)
    places = places.astype(jnp.int32)
    firsts, seconds = gather_sections(first, second, weights)
    results = products(places, weights[1], FIRST, seconds)
    return tuple(products(places, weights[0], 0, firsts, results))


def solution(mesh):
    fine = Mesh(mesh.devices.reshape(NX, 2, 2, 4, 2), SECT + DEV)
    return jax.shard_map(
        local,
        mesh=fine,
        in_specs=(P(None, SECT, DEV), P(), P(SECT), P(SECT), P(SECT, None)),
        out_specs=(P(None, DEV, SECT, None), P(None, DEV, SECT, None)),
        check_vma=False,
    )
```

```python
import functools
import math

import jax
import jax.numpy as jnp
import numpy as np
from jax import lax
from jax.experimental import pallas as pl
from jax.experimental.pallas import tpu as pltpu
from jax.sharding import Mesh
from jax.sharding import PartitionSpec as P

FEEDS = 2048
CHANNELS = 1024
TILES = 128
TAPS = 4
FRAMES = 128

SECT = ("x", "yh")
DEV = ("yl", "z", "core")
NX = 4
PER = 16
LOCAL_FRAMES = 8
LATE = 3
EARLY = LOCAL_FRAMES - LATE
LOCAL_CHANS = 64
FIRST = 40
BF16 = jnp.bfloat16
F32 = jnp.float32


def ring(v, by):
    return lax.ppermute(v, "x", [(i, (i + by) % NX) for i in range(NX)])


def pair(v):
    return lax.ppermute(v, "yh", [(0, 1), (1, 0)])


def params(mib):
    return pltpu.CompilerParams(vmem_limit_bytes=mib * 1024 * 1024)


IN_VMEM = pl.BlockSpec(memory_space=pltpu.VMEM)
IN_SMEM = pl.BlockSpec(memory_space=pltpu.SMEM)
ANYWHERE = pl.BlockSpec(memory_space=pl.ANY)
IN_HBM = pl.BlockSpec(memory_space=pltpu.HBM)


def combine_kernel(layout, *refs):
    in_refs, out_refs = refs[: -len(layout)], refs[-len(layout) :]
    for out_ref, blocks in zip(out_refs, layout):
        for place, terms in enumerate(blocks):
            values = [in_refs[array][index] for array, index in terms]
            if len(values) > 1:
                total = values[0].astype(F32)
                for value in values[1:]:
                    total = total + value.astype(F32)
                values = [total.astype(BF16)]
            out_ref[place] = values[0]


def combine(arrays, layout, others=()):
    shapes = []
    for blocks in layout:
        array, index = blocks[0][0]
        shapes.append((len(blocks),) + jax.eval_shape(lambda a, index=index: a[index], arrays[array]).shape)
    return pl.pallas_call(
        functools.partial(combine_kernel, layout),
        in_specs=[IN_VMEM] * len(arrays) + [ANYWHERE] * len(others),
        out_specs=[IN_VMEM] * len(layout),
        out_shape=[jax.ShapeDtypeStruct(shape, BF16) for shape in shapes],
        compiler_params=params(4),
        cost_estimate=pl.CostEstimate(flops=1000, bytes_accessed=1000000, transcendentals=0),
    )(*arrays, *others)


def tile_sums_kernel(first, frames, groups, member_ref, volts_ref, *refs):
    out_refs, (chunk_ref, sems) = refs[-2 - len(groups) : -2], refs[-2:]
    copies = [
        pltpu.make_async_copy(
            volts_ref.at[z, :, pl.ds((first + t) * CHANNELS, CHANNELS)],
            chunk_ref.at[t, z],
            sems.at[t, z],
        )
        for t in range(frames)
        for z in range(2)
    ]
    for copy in copies:
        copy.start()
    for t in range(frames):
        for z in range(2):
            copies[t * 2 + z].wait()
            sums = jnp.dot(member_ref[...], chunk_ref[t, z], preferred_element_type=F32).astype(BF16)
            for out_ref, group in zip(out_refs, groups):
                for place, block in enumerate(group):
                    out_ref[place, t, z] = sums[block * PER : (block + 1) * PER]


def tile_sums(member, voltages, first, frames, groups, others=()):
    feeds = voltages.shape[1]
    return pl.pallas_call(
        functools.partial(tile_sums_kernel, first, frames, groups),
        in_specs=[IN_VMEM, IN_HBM] + [ANYWHERE] * len(others),
        out_specs=[IN_VMEM] * len(groups),
        out_shape=[jax.ShapeDtypeStruct((len(g), frames, 2, PER, CHANNELS), BF16) for g in groups],
        scratch_shapes=[
            pltpu.VMEM((frames, 2, feeds, CHANNELS), BF16),
            pltpu.SemaphoreType.DMA((frames, 2)),
        ],
        compiler_params=params(50),
        cost_estimate=pl.CostEstimate(
            flops=2 * TILES * feeds * CHANNELS * 2 * frames,
            bytes_accessed=2 * 2 * frames * CHANNELS * (feeds + TILES) * 2,
            transcendentals=0,
        ),
    )(member, voltages, *others)


def weights_kernel(base_ref, delays_ref, out_ref):
    @pl.loop(0, out_ref.shape[0])
    def _(c):
        channel = (base_ref[0] + c).astype(F32)
        quarters = (delays_ref[...] * channel) * (4.0 / CHANNELS)
        near = jnp.floor(quarters + 0.5)
        rest = quarters - near
        square = rest * rest
        sine = rest * (
            1.5707963267948966
            + square * (-0.6459640975062462 + square * (0.07969262624616703 + square * -0.004681754135318687))
        )
        cosine = 1.0 + square * (
            -1.2337005501361697
            + square * (0.253669507901048 + square * (-0.020863480763353 + square * 0.000919260274839426))
        )
        turn = near.astype(jnp.int32) & 3
        odd = (turn & 1) == 1
        cos_value, sin_value = jnp.where(odd, sine, cosine), jnp.where(odd, cosine, sine)
        cos_value = jnp.where((turn == 1) | (turn == 2), -cos_value, cos_value)
        sin_value = jnp.where(turn >= 2, -sin_value, sin_value)
        out_ref[c, :, 0:TILES] = cos_value.astype(BF16)
        out_ref[c, :, TILES : 2 * TILES] = sin_value.astype(BF16)


def beam_weights(base, delays, count):
    beams = delays.shape[0]
    return pl.pallas_call(
        weights_kernel,
        in_specs=[IN_SMEM, IN_VMEM],
        out_specs=IN_VMEM,
        out_shape=jax.ShapeDtypeStruct((count, beams, 2 * TILES), BF16),
        compiler_params=params(4),
        cost_estimate=pl.CostEstimate(
            flops=1000, bytes_accessed=count * 400 * 1024, transcendentals=0
        ),
    )(jnp.reshape(base, (1,)), delays)


def spectra_kernel(early_refs, late_ref, past_ref, taps_ref, cos_ref, sin_ref, out_ref, filt_ref):
    def frame(t, z):
        if t < 0:
            return past_ref[t + LATE, z].astype(F32)
        if t < EARLY:
            return early_refs[0][0, t, z].astype(F32) + early_refs[1][0, t, z].astype(F32)
        return late_ref[t - EARLY, z].astype(F32)

    for z in range(2):
        for t in range(LOCAL_FRAMES):
            total = taps_ref[0:1, :] * frame(t, z)
            for m in range(1, TAPS):
                total = total + taps_ref[m : m + 1, :] * frame(t - m, z)
            filt_ref[z * TILES + t * PER : z * TILES + (t + 1) * PER, :] = total.astype(BF16)

    block = 256
    for begin in range(0, CHANNELS, block):
        columns = slice(begin, begin + block)
        by_cos = jnp.dot(filt_ref[...], cos_ref[:, columns], preferred_element_type=F32)
        by_sin = jnp.dot(filt_ref[...], sin_ref[:, columns], preferred_element_type=F32)
        real = by_cos[0:128] + by_sin[128:256]
        quad = by_cos[128:256] - by_sin[0:128]
        for n in range(block // 128):
            lanes = slice(n * 128, (n + 1) * 128)
            own, other = real[:, lanes], quad[:, lanes]
            place = begin // LOCAL_CHANS + 2 * n
            out_ref[place] = jnp.concatenate([own[:, 0:64], other[:, 0:64]], axis=1).astype(BF16)
            out_ref[place + 1] = jnp.concatenate([own[:, 64:128], other[:, 64:128]], axis=1).astype(BF16)


def spectra(early, late, past, taps, cos_table, sin_table):
    def kernel(own_ref, got_ref, late_ref, past_ref, taps_ref, cos_ref, sin_ref, out_ref, filt_ref):
        spectra_kernel((own_ref, got_ref), late_ref, past_ref, taps_ref, cos_ref, sin_ref, out_ref, filt_ref)

    return pl.pallas_call(
        kernel,
        in_specs=[IN_VMEM] * 7,
        out_specs=IN_VMEM,
        out_shape=jax.ShapeDtypeStruct((CHANNELS // LOCAL_CHANS, TILES, 128), BF16),
        scratch_shapes=[pltpu.VMEM((256, CHANNELS), BF16)],
        compiler_params=params(12),
        cost_estimate=pl.CostEstimate(
            flops=2 * 2 * 256 * CHANNELS * CHANNELS, bytes_accessed=6 * 1024 * 1024, transcendentals=0
        ),
    )(*early, late, past, taps, cos_table, sin_table)


def turn_kernel(in_ref, first_ref, second_ref, wide_ref, turned_ref):
    for d in range(in_ref.shape[0]):
        wide_ref[d * TILES : (d + 1) * TILES] = in_ref[d].astype(F32)
    for a in range(PER):
        turned_ref[pl.ds(a, 128, stride=PER)] = wide_ref[pl.ds(a, 128, stride=PER)].T
    for z in range(2):
        for ref, begin in ((first_ref, 0), (second_ref, FIRST)):
            for c in range(ref.shape[0]):
                row = (z * LOCAL_CHANS + begin + c) * PER
                ref[c, z] = turned_ref[row : row + PER].astype(BF16)


def turn(value):
    return pl.pallas_call(
        turn_kernel,
        in_specs=[IN_VMEM],
        out_specs=[IN_VMEM] * 2,
        out_shape=[jax.ShapeDtypeStruct((n, 2, PER, FRAMES), BF16) for n in (FIRST, LOCAL_CHANS - FIRST)],
        scratch_shapes=[pltpu.VMEM((FRAMES * PER, 128), F32)] * 2,
        compiler_params=params(4),
        cost_estimate=pl.CostEstimate(flops=1000, bytes_accessed=4000000, transcendentals=0),
    )(value)


def products_kernel(begin, blocks, places_ref, weight_ref, block_refs, vis_ref, beam_ref, both_ref, vis_out, beam_out, vis_sem, beam_sem):
    vis_scale = 1.0 / (FRAMES * FEEDS / TILES)
    beam_scale = 1.0 / math.sqrt(FEEDS)
    dims = (((1,), (1,)), ((), ()))
    each = both_ref.shape[0]
    steps = weight_ref.shape[0] // each

    def copies(step):
        here, there = pl.ds(step * each, each), pl.ds(begin + step * each, each)
        return [
            pltpu.make_async_copy(source.at[z, here], target.at[z, there], sem.at[z, step])
            for source, target, sem in ((vis_out, vis_ref, vis_sem), (beam_out, beam_ref, beam_sem))
            for z in range(2)
        ]

    @pl.loop(0, steps)
    def _(step):
        for c in range(each):
            here = step * each + c
            for place, (array, index) in enumerate(blocks):
                row = pl.multiple_of(places_ref[place] * PER, PER)
                real, quad = block_refs[array][index, here, 0], block_refs[array][index, here, 1]
                both_ref[c, pl.ds(row, PER), 0:128] = real
                both_ref[c, pl.ds(row, PER), 128:256] = quad
                both_ref[c, pl.ds(TILES + row, PER), 0:128] = quad
                both_ref[c, pl.ds(TILES + row, PER), 128:256] = -real
        for c in range(each):
            here = step * each + c
            beams = jnp.dot(weight_ref[here], both_ref[c], preferred_element_type=F32) * beam_scale
            beam_out[0, here] = beams[:, 0:128].astype(BF16)
            beam_out[1, here] = beams[:, 128:256].astype(BF16)
            array, index = blocks[0]
            real, quad = block_refs[array][index, here, 0], block_refs[array][index, here, 1]
            mine = jnp.concatenate(
                [jnp.concatenate([real, quad], axis=1), jnp.concatenate([quad, -real], axis=1)], axis=0
            )
            vis = lax.dot_general(mine, both_ref[c, 0:TILES], dims, preferred_element_type=F32) * vis_scale
            vis_out[0, here] = vis[:PER]
            vis_out[1, here] = vis[PER:]
        for copy in copies(step):
            copy.start()

    @pl.loop(0, steps)
    def _(step):
        for copy in copies(step):
            copy.wait()


def products(places, weights, begin, blocks, results=()):
    arrays, layout = [], []
    for array, index in blocks:
        if not any(array is a for a in arrays):
            arrays.append(array)
        layout.append((next(n for n, a in enumerate(arrays) if a is array), index))
    count, beams = weights.shape[:2]
    each = next(n for n in (10, 8) if count % n == 0)

    def kernel(places_ref, weight_ref, *refs):
        products_kernel(begin, layout, places_ref, weight_ref, refs[: len(arrays)], *refs[len(arrays) + len(results) :])

    return pl.pallas_call(
        kernel,
        in_specs=[IN_SMEM] + [IN_VMEM] * (1 + len(arrays)) + [IN_HBM] * len(results),
        out_specs=[IN_HBM, IN_HBM],
        out_shape=[
            jax.ShapeDtypeStruct((2, LOCAL_CHANS, PER, TILES), F32),
            jax.ShapeDtypeStruct((2, LOCAL_CHANS, beams, FRAMES), BF16),
        ],
        scratch_shapes=[
            pltpu.VMEM((each, 2 * TILES, 256), BF16),
            pltpu.VMEM((2, count, PER, TILES), F32),
            pltpu.VMEM((2, count, beams, FRAMES), BF16),
            pltpu.SemaphoreType.DMA((2, count // each)),
            pltpu.SemaphoreType.DMA((2, count // each)),
        ],
        input_output_aliases={2 + len(arrays) + n: n for n in range(len(results))},
        compiler_params=params(8),
        cost_estimate=pl.CostEstimate(
            flops=2 * count * 160 * 256 * 256, bytes_accessed=count * 400 * 1024, transcendentals=0
        ),
    )(places, weights, *arrays, *results)


def reduce_sections(member, voltages):
    x_plus, x_minus, x_rest = tile_sums(member, voltages, 0, EARLY, ((4, 3), (5, 6), (0, 1, 2, 7)))
    keep, give = tile_sums(member, voltages, EARLY, LATE, ((0, 2, 4, 6), (1, 3, 5, 7)), (x_rest,))
    got = pair(give)
    from_minus, from_plus = ring(x_plus, 1), ring(x_minus, -1)
    x_next, x_prev = combine(
        (x_rest, from_minus, from_plus), ([[(0, 2), (1, 0)]], [[(0, 3), (2, 0)]])
    )
    last_minus, last_plus = ring(x_next, 1), ring(x_prev, -1)
    early_own, early_give = combine(
        (x_rest, last_minus, last_plus, from_minus, from_plus),
        ([[(0, 0), (1, 0), (4, 1)]], [[(0, 1), (2, 0), (3, 1)]]),
    )
    early = (early_own, pair(early_give))

    y_own, y_next, y_far, y_prev = combine(
        (keep, got), [[[(0, (rx, t)), (1, (rx, t))] for t in range(LATE)] for rx in range(NX)]
    )
    (late,) = combine(
        (y_own, ring(y_next, 1), ring(y_far, 2), ring(y_prev, 3)),
        ([[(n, t) for n in range(NX)] for t in range(LATE)],),
    )
    return early, late


def gather_sections(first, second, others):
    (both,) = combine((first, pair(first)), ([[(0, slice(None))], [(1, slice(None))]],))
    both_minus, both_plus = ring(both, 1), ring(both, -1)
    own_far, pair_far = combine((both_minus, both_plus), ([[(0, 0)]], [[(1, 1)]]), others)
    own_far, pair_far = ring(own_far, 1), ring(pair_far, -1)
    firsts = ((both, 0), (both, 1), (both_plus, 0), (both_plus, 1))
    firsts += ((own_far, 0), (pair_far, 0), (both_minus, 0), (both_minus, 1))

    (mine,) = combine(
        (second, ring(second, -1), ring(second, 2), ring(second, 1)), ([[(n, slice(None))] for n in range(NX)],)
    )
    theirs = pair(mine)
    seconds = tuple((v, n) for n in range(NX) for v in (mine, theirs))
    return firsts, seconds


def fourier_tables():
    positions = np.arange(CHANNELS, dtype=np.int64)
    angle = (positions[:, None] * positions[None, :] % CHANNELS) * (2.0 * math.pi / CHANNELS)
    factor = 1.0 / math.sqrt(CHANNELS)
    cos_table = (np.cos(angle) * factor).astype(np.float32).astype(BF16)
    sin_table = (np.sin(angle) * factor).astype(np.float32).astype(BF16)
    return jnp.asarray(cos_table), jnp.asarray(sin_table)


def local(voltages, filter_taps, feed_tile, bad_feed, delays):
    x, y = lax.axis_index("x"), lax.axis_index("yh")
    section = feed_tile // PER
    place = (((section // 2 - x) % NX) * 2 + (section % 2 ^ y)) * PER + feed_tile % PER
    place = jnp.where(bad_feed == 0, place, -1)
    member = (jnp.arange(TILES, dtype=jnp.int32)[:, None] == place[None, :]).astype(BF16)
    cos_table, sin_table = fourier_tables()
    base = (lax.axis_index(DEV) * LOCAL_CHANS).astype(jnp.int32)
    counts = (FIRST, LOCAL_CHANS - FIRST)
    weights = [beam_weights(base + b, delays, n) for b, n in zip((0, FIRST), counts)]

    early, late = reduce_sections(member, voltages)
    past = lax.ppermute(late, DEV, [(i, i + 1) for i in range(FRAMES // LOCAL_FRAMES - 1)])
    spec = spectra(early, late, past, filter_taps, cos_table, sin_table)
    first, second = turn(lax.all_to_all(spec, DEV, 0, 0, tiled=True))
    rel = jnp.arange(8, dtype=jnp.int32)
    places = ((x + rel // 2) % NX) * 2 + (rel % 2 ^ y)
    places = places.astype(jnp.int32)
    firsts, seconds = gather_sections(first, second, weights)
    results = products(places, weights[1], FIRST, seconds)
    return tuple(products(places, weights[0], 0, firsts, results))


def solution(mesh):
    fine = Mesh(mesh.devices.reshape(NX, 2, 2, 4, 2), SECT + DEV)
    return jax.shard_map(
        local,
        mesh=fine,
        in_specs=(P(None, SECT, DEV), P(), P(SECT), P(SECT), P(SECT, None)),
        out_specs=(P(None, DEV, SECT, None), P(None, DEV, SECT, None)),
        check_vma=False,
    )
```

```python
import functools
import math

import jax
import jax.numpy as jnp
import numpy as np
from jax import lax
from jax.experimental import pallas as pl
from jax.experimental.pallas import tpu as pltpu
from jax.sharding import Mesh
from jax.sharding import PartitionSpec as P

FEEDS = 2048
CHANNELS = 1024
TILES = 128
TAPS = 4
FRAMES = 128

SECT = ("x", "yh")
DEV = ("yl", "z", "core")
NX = 4
PER = 16
LOCAL_FRAMES = 8
LATE = 3
EARLY = LOCAL_FRAMES - LATE
LOCAL_CHANS = 64
FIRST = 44
BF16 = jnp.bfloat16
F32 = jnp.float32


def ring(v, by):
    return lax.ppermute(v, "x", [(i, (i + by) % NX) for i in range(NX)])


def pair(v):
    return lax.ppermute(v, "yh", [(0, 1), (1, 0)])


def params(mib):
    return pltpu.CompilerParams(vmem_limit_bytes=mib * 1024 * 1024)


IN_VMEM = pl.BlockSpec(memory_space=pltpu.VMEM)
IN_SMEM = pl.BlockSpec(memory_space=pltpu.SMEM)
ANYWHERE = pl.BlockSpec(memory_space=pl.ANY)
IN_HBM = pl.BlockSpec(memory_space=pltpu.HBM)


def combine_kernel(layout, *refs):
    in_refs, out_refs = refs[: -len(layout)], refs[-len(layout) :]
    for out_ref, blocks in zip(out_refs, layout):
        for place, terms in enumerate(blocks):
            values = [in_refs[array][index] for array, index in terms]
            if len(values) > 1:
                total = values[0].astype(F32)
                for value in values[1:]:
                    total = total + value.astype(F32)
                values = [total.astype(BF16)]
            out_ref[place] = values[0]


def combine(arrays, layout, others=()):
    shapes = []
    for blocks in layout:
        array, index = blocks[0][0]
        shapes.append((len(blocks),) + jax.eval_shape(lambda a, index=index: a[index], arrays[array]).shape)
    return pl.pallas_call(
        functools.partial(combine_kernel, layout),
        in_specs=[IN_VMEM] * len(arrays) + [ANYWHERE] * len(others),
        out_specs=[IN_VMEM] * len(layout),
        out_shape=[jax.ShapeDtypeStruct(shape, BF16) for shape in shapes],
        compiler_params=params(4),
        cost_estimate=pl.CostEstimate(flops=1000, bytes_accessed=1000000, transcendentals=0),
    )(*arrays, *others)


def tile_sums_kernel(first, frames, groups, member_ref, volts_ref, *refs):
    out_refs, (chunk_ref, sems) = refs[-2 - len(groups) : -2], refs[-2:]
    copies = [
        pltpu.make_async_copy(
            volts_ref.at[z, :, pl.ds((first + t) * CHANNELS, CHANNELS)],
            chunk_ref.at[t, z],
            sems.at[t, z],
        )
        for t in range(frames)
        for z in range(2)
    ]
    for copy in copies:
        copy.start()
    for t in range(frames):
        for z in range(2):
            copies[t * 2 + z].wait()
            sums = jnp.dot(member_ref[...], chunk_ref[t, z], preferred_element_type=F32).astype(BF16)
            for out_ref, group in zip(out_refs, groups):
                for place, block in enumerate(group):
                    out_ref[place, t, z] = sums[block * PER : (block + 1) * PER]


def tile_sums(member, voltages, first, frames, groups, others=()):
    feeds = voltages.shape[1]
    return pl.pallas_call(
        functools.partial(tile_sums_kernel, first, frames, groups),
        in_specs=[IN_VMEM, IN_HBM] + [ANYWHERE] * len(others),
        out_specs=[IN_VMEM] * len(groups),
        out_shape=[jax.ShapeDtypeStruct((len(g), frames, 2, PER, CHANNELS), BF16) for g in groups],
        scratch_shapes=[
            pltpu.VMEM((frames, 2, feeds, CHANNELS), BF16),
            pltpu.SemaphoreType.DMA((frames, 2)),
        ],
        compiler_params=params(50),
        cost_estimate=pl.CostEstimate(
            flops=2 * TILES * feeds * CHANNELS * 2 * frames,
            bytes_accessed=2 * 2 * frames * CHANNELS * (feeds + TILES) * 2,
            transcendentals=0,
        ),
    )(member, voltages, *others)


def weights_kernel(base_ref, delays_ref, out_ref):
    @pl.loop(0, out_ref.shape[0])
    def _(c):
        channel = (base_ref[0] + c).astype(F32)
        quarters = (delays_ref[...] * channel) * (4.0 / CHANNELS)
        near = jnp.floor(quarters + 0.5)
        rest = quarters - near
        square = rest * rest
        sine = rest * (
            1.5707963267948966
            + square * (-0.6459640975062462 + square * (0.07969262624616703 + square * -0.004681754135318687))
        )
        cosine = 1.0 + square * (
            -1.2337005501361697
            + square * (0.253669507901048 + square * (-0.020863480763353 + square * 0.000919260274839426))
        )
        turn = near.astype(jnp.int32) & 3
        odd = (turn & 1) == 1
        cos_value, sin_value = jnp.where(odd, sine, cosine), jnp.where(odd, cosine, sine)
        cos_value = jnp.where((turn == 1) | (turn == 2), -cos_value, cos_value)
        sin_value = jnp.where(turn >= 2, -sin_value, sin_value)
        out_ref[c, :, 0:TILES] = cos_value.astype(BF16)
        out_ref[c, :, TILES : 2 * TILES] = sin_value.astype(BF16)


def beam_weights(base, delays, count):
    beams = delays.shape[0]
    return pl.pallas_call(
        weights_kernel,
        in_specs=[IN_SMEM, IN_VMEM],
        out_specs=IN_VMEM,
        out_shape=jax.ShapeDtypeStruct((count, beams, 2 * TILES), BF16),
        compiler_params=params(4),
        cost_estimate=pl.CostEstimate(
            flops=1000, bytes_accessed=count * 400 * 1024, transcendentals=0
        ),
    )(jnp.reshape(base, (1,)), delays)


def spectra_kernel(early_refs, late_ref, past_ref, taps_ref, cos_ref, sin_ref, out_ref, filt_ref):
    def frame(t, z):
        if t < 0:
            return past_ref[t + LATE, z].astype(F32)
        if t < EARLY:
            return early_refs[0][0, t, z].astype(F32) + early_refs[1][0, t, z].astype(F32)
        return late_ref[t - EARLY, z].astype(F32)

    for z in range(2):
        for t in range(LOCAL_FRAMES):
            total = taps_ref[0:1, :] * frame(t, z)
            for m in range(1, TAPS):
                total = total + taps_ref[m : m + 1, :] * frame(t - m, z)
            filt_ref[z * TILES + t * PER : z * TILES + (t + 1) * PER, :] = total.astype(BF16)

    block = 256
    for begin in range(0, CHANNELS, block):
        columns = slice(begin, begin + block)
        by_cos = jnp.dot(filt_ref[...], cos_ref[:, columns], preferred_element_type=F32)
        by_sin = jnp.dot(filt_ref[...], sin_ref[:, columns], preferred_element_type=F32)
        real = by_cos[0:128] + by_sin[128:256]
        quad = by_cos[128:256] - by_sin[0:128]
        for n in range(block // 128):
            lanes = slice(n * 128, (n + 1) * 128)
            own, other = real[:, lanes], quad[:, lanes]
            place = begin // LOCAL_CHANS + 2 * n
            out_ref[place] = jnp.concatenate([own[:, 0:64], other[:, 0:64]], axis=1).astype(BF16)
            out_ref[place + 1] = jnp.concatenate([own[:, 64:128], other[:, 64:128]], axis=1).astype(BF16)


def spectra(early, late, past, taps, cos_table, sin_table):
    def kernel(own_ref, got_ref, late_ref, past_ref, taps_ref, cos_ref, sin_ref, out_ref, filt_ref):
        spectra_kernel((own_ref, got_ref), late_ref, past_ref, taps_ref, cos_ref, sin_ref, out_ref, filt_ref)

    return pl.pallas_call(
        kernel,
        in_specs=[IN_VMEM] * 7,
        out_specs=IN_VMEM,
        out_shape=jax.ShapeDtypeStruct((CHANNELS // LOCAL_CHANS, TILES, 128), BF16),
        scratch_shapes=[pltpu.VMEM((256, CHANNELS), BF16)],
        compiler_params=params(12),
        cost_estimate=pl.CostEstimate(
            flops=2 * 2 * 256 * CHANNELS * CHANNELS, bytes_accessed=6 * 1024 * 1024, transcendentals=0
        ),
    )(*early, late, past, taps, cos_table, sin_table)


def turn_kernel(in_ref, first_ref, second_ref, wide_ref, turned_ref):
    for d in range(in_ref.shape[0]):
        wide_ref[d * TILES : (d + 1) * TILES] = in_ref[d].astype(F32)
    for a in range(PER):
        turned_ref[pl.ds(a, 128, stride=PER)] = wide_ref[pl.ds(a, 128, stride=PER)].T
    for z in range(2):
        for ref, begin in ((first_ref, 0), (second_ref, FIRST)):
            for c in range(ref.shape[0]):
                row = (z * LOCAL_CHANS + begin + c) * PER
                ref[c, z] = turned_ref[row : row + PER].astype(BF16)


def turn(value):
    return pl.pallas_call(
        turn_kernel,
        in_specs=[IN_VMEM],
        out_specs=[IN_VMEM] * 2,
        out_shape=[jax.ShapeDtypeStruct((n, 2, PER, FRAMES), BF16) for n in (FIRST, LOCAL_CHANS - FIRST)],
        scratch_shapes=[pltpu.VMEM((FRAMES * PER, 128), F32)] * 2,
        compiler_params=params(4),
        cost_estimate=pl.CostEstimate(flops=1000, bytes_accessed=4000000, transcendentals=0),
    )(value)


def products_kernel(begin, blocks, places_ref, weight_ref, block_refs, vis_ref, beam_ref, both_ref, vis_out, beam_out, vis_sem, beam_sem):
    vis_scale = 1.0 / (FRAMES * FEEDS / TILES)
    beam_scale = 1.0 / math.sqrt(FEEDS)
    dims = (((1,), (1,)), ((), ()))
    each = both_ref.shape[0]
    steps = weight_ref.shape[0] // each

    def copies(step):
        here, there = pl.ds(step * each, each), pl.ds(begin + step * each, each)
        return [
            pltpu.make_async_copy(source.at[z, here], target.at[z, there], sem.at[z, step])
            for source, target, sem in ((vis_out, vis_ref, vis_sem), (beam_out, beam_ref, beam_sem))
            for z in range(2)
        ]

    def load(pieces, part, here):
        array, index = pieces[part % len(pieces)]
        if len(pieces) > 1:
            here = here - part * (steps // 2) * each
        return [block_refs[array][(*index, here, z)] for z in range(2)]

    def work(part, step):
        for c in range(each):
            here = step * each + c
            for place, pieces in enumerate(blocks):
                row = pl.multiple_of(places_ref[place] * PER, PER)
                real, quad = load(pieces, part, here)
                both_ref[c, pl.ds(row, PER), 0:128] = real
                both_ref[c, pl.ds(row, PER), 128:256] = quad
                both_ref[c, pl.ds(TILES + row, PER), 0:128] = quad
                both_ref[c, pl.ds(TILES + row, PER), 128:256] = -real
        for c in range(each):
            here = step * each + c
            beams = jnp.dot(weight_ref[here], both_ref[c], preferred_element_type=F32) * beam_scale
            beam_out[0, here] = beams[:, 0:128].astype(BF16)
            beam_out[1, here] = beams[:, 128:256].astype(BF16)
            real, quad = load(blocks[0], part, here)
            mine = jnp.concatenate(
                [jnp.concatenate([real, quad], axis=1), jnp.concatenate([quad, -real], axis=1)], axis=0
            )
            vis = lax.dot_general(mine, both_ref[c, 0:TILES], dims, preferred_element_type=F32) * vis_scale
            vis_out[0, here] = vis[:PER]
            vis_out[1, here] = vis[PER:]
        for copy in copies(step):
            copy.start()

    pl.loop(0, steps // 2)(functools.partial(work, 0))
    pl.loop(steps // 2, steps)(functools.partial(work, 1))

    @pl.loop(0, steps)
    def _(step):
        for copy in copies(step):
            copy.wait()


def products(places, weights, begin, blocks, results=()):
    arrays, layout = [], []
    for pieces in blocks:
        layout.append([])
        for array, index in pieces:
            if not any(array is a for a in arrays):
                arrays.append(array)
            layout[-1].append((next(n for n, a in enumerate(arrays) if a is array), index))
    count, beams = weights.shape[:2]
    each = next(n for n in (11, 10) if count % n == 0)

    def kernel(places_ref, weight_ref, *refs):
        products_kernel(begin, layout, places_ref, weight_ref, refs[: len(arrays)], *refs[len(arrays) + len(results) :])

    return pl.pallas_call(
        kernel,
        in_specs=[IN_SMEM] + [IN_VMEM] * (1 + len(arrays)) + [IN_HBM] * len(results),
        out_specs=[IN_HBM, IN_HBM],
        out_shape=[
            jax.ShapeDtypeStruct((2, LOCAL_CHANS, PER, TILES), F32),
            jax.ShapeDtypeStruct((2, LOCAL_CHANS, beams, FRAMES), BF16),
        ],
        scratch_shapes=[
            pltpu.VMEM((each, 2 * TILES, 256), BF16),
            pltpu.VMEM((2, count, PER, TILES), F32),
            pltpu.VMEM((2, count, beams, FRAMES), BF16),
            pltpu.SemaphoreType.DMA((2, count // each)),
            pltpu.SemaphoreType.DMA((2, count // each)),
        ],
        input_output_aliases={2 + len(arrays) + n: n for n in range(len(results))},
        compiler_params=params(8),
        cost_estimate=pl.CostEstimate(
            flops=2 * count * 160 * 256 * 256, bytes_accessed=count * 400 * 1024, transcendentals=0
        ),
    )(places, weights, *arrays, *results)


def reduce_sections(member, voltages):
    x_plus, x_minus, x_rest = tile_sums(member, voltages, 0, EARLY, ((4, 3), (5, 6), (0, 1, 2, 7)))
    keep, give = tile_sums(member, voltages, EARLY, LATE, ((0, 2, 4, 6), (1, 3, 5, 7)), (x_rest,))
    got = pair(give)
    from_minus, from_plus = ring(x_plus, 1), ring(x_minus, -1)
    x_next, x_prev = combine(
        (x_rest, from_minus, from_plus), ([[(0, 2), (1, 0)]], [[(0, 3), (2, 0)]])
    )
    last_minus, last_plus = ring(x_next, 1), ring(x_prev, -1)
    early_own, early_give = combine(
        (x_rest, last_minus, last_plus, from_minus, from_plus),
        ([[(0, 0), (1, 0), (4, 1)]], [[(0, 1), (2, 0), (3, 1)]]),
    )
    early = (early_own, pair(early_give))

    y_own, y_next, y_far, y_prev = combine(
        (keep, got), [[[(0, (rx, t)), (1, (rx, t))] for t in range(LATE)] for rx in range(NX)]
    )
    (late,) = combine(
        (y_own, ring(y_next, 1), ring(y_far, 2), ring(y_prev, 3)),
        ([[(n, t) for n in range(NX)] for t in range(LATE)],),
    )
    return early, late


def gather_sections(first, second, others):
    half = first.shape[0] // 2
    low, high = slice(0, half), slice(half, None)
    own = [ring(first, by) for by in (1, -1)]
    first_pair = pair(first)
    pairs = [ring(first_pair, by) for by in (1, -1)]
    far = []
    for minus, plus, needed in (own + [()], pairs + [others]):
        parts = combine((minus, plus), ([[(0, n)] for n in range(half)], [[(1, half + n)] for n in range(half)]), needed)
        far.append((ring(parts[0], 1), ring(parts[1], -1)))
    firsts = [(first,), (first_pair,), (own[1],), (pairs[1],), far[0], far[1], (own[0],), (pairs[0],)]
    firsts = [[(v, ()) for v in pieces] for pieces in firsts]

    (mine,) = combine(
        (second, ring(second, -1), ring(second, 2), ring(second, 1)), ([[(n, slice(None))] for n in range(NX)],)
    )
    theirs = pair(mine)
    seconds = [[(v, (n,))] for n in range(NX) for v in (mine, theirs)]
    return firsts, seconds


def fourier_tables():
    positions = np.arange(CHANNELS, dtype=np.int64)
    angle = (positions[:, None] * positions[None, :] % CHANNELS) * (2.0 * math.pi / CHANNELS)
    factor = 1.0 / math.sqrt(CHANNELS)
    cos_table = (np.cos(angle) * factor).astype(np.float32).astype(BF16)
    sin_table = (np.sin(angle) * factor).astype(np.float32).astype(BF16)
    return jnp.asarray(cos_table), jnp.asarray(sin_table)


def local(voltages, filter_taps, feed_tile, bad_feed, delays):
    x, y = lax.axis_index("x"), lax.axis_index("yh")
    section = feed_tile // PER
    place = (((section // 2 - x) % NX) * 2 + (section % 2 ^ y)) * PER + feed_tile % PER
    place = jnp.where(bad_feed == 0, place, -1)
    member = (jnp.arange(TILES, dtype=jnp.int32)[:, None] == place[None, :]).astype(BF16)
    cos_table, sin_table = fourier_tables()
    base = (lax.axis_index(DEV) * LOCAL_CHANS).astype(jnp.int32)
    counts = (FIRST, LOCAL_CHANS - FIRST)
    weights = [beam_weights(base + b, delays, n) for b, n in zip((0, FIRST), counts)]

    early, late = reduce_sections(member, voltages)
    past = lax.ppermute(late, DEV, [(i, i + 1) for i in range(FRAMES // LOCAL_FRAMES - 1)])
    spec = spectra(early, late, past, filter_taps, cos_table, sin_table)
    first, second = turn(lax.all_to_all(spec, DEV, 0, 0, tiled=True))
    rel = jnp.arange(8, dtype=jnp.int32)
    places = ((x + rel // 2) % NX) * 2 + (rel % 2 ^ y)
    places = places.astype(jnp.int32)
    firsts, seconds = gather_sections(first, second, weights)
    results = products(places, weights[1], FIRST, seconds)
    return tuple(products(places, weights[0], 0, firsts, results))


def solution(mesh):
    fine = Mesh(mesh.devices.reshape(NX, 2, 2, 4, 2), SECT + DEV)
    return jax.shard_map(
        local,
        mesh=fine,
        in_specs=(P(None, SECT, DEV), P(), P(SECT), P(SECT), P(SECT, None)),
        out_specs=(P(None, DEV, SECT, None), P(None, DEV, SECT, None)),
        check_vma=False,
    )
```
